32 devices in a mesh: groups: 2 (over y), rows: 4 (over z), cols: 4 (over x, core).
Axes of the slice: x: 2, y: 2, z: 4, core: 2. Of those that a mesh axis runs over, the one named last changes fastest.
Arguments:
- iterate: bfloat16 [4096, 2048], P(('groups', 'rows'), 'cols'), parts along dimension 0, may hold values from -6 to 6
- square: bfloat16 [4096, 2048], P(('groups', 'rows'), 'cols'), parts along dimension 0, may hold values from -0.5 to 0.5
- iterate_pattern: int32 [32, 16], P(('groups', 'rows'), 'cols'), parts along dimension 0, may hold values from 0 to 1, as said below
- square_pattern: int32 [32, 16], P(('groups', 'rows'), 'cols'), parts along dimension 0, may hold values from 0 to 1, as said below
- keep_pattern: int32 [32, 16], P(('groups', 'rows'), 'cols'), parts along dimension 0, may hold values 0 or 1
Outputs:
- next_iterate: float32 [4096, 2048], P(('groups', 'rows'), 'cols'), parts along dimension 0
The draws below stay inside these ranges and needn't reach their ends.
There are 2 independent parts, one for each index of `groups`. The reference program is written for one: setup_inputs(seed, part) draws one part's arguments, and reference() takes and returns one part's arrays. A program takes and returns all parts, laid end to end along the dimension named above; each array names one. Nothing has to cross between parts.
Inputs may be any that keep to these rules, and one draw needn't show every extreme that they name: `iterate_pattern`: in each aligned tile of 4 x 4 blocks (block rows k * 4 to k * 4 + 3, block columns likewise) at most 4 blocks are stored, and at least one; some tile holds exactly 4. `square_pattern`: in each aligned tile of 4 x 4 blocks at most 4 blocks are stored, and at least one; some tile holds exactly 4.
All inputs are finite; a program needn't handle non-finite values. No bound on the sum of `keep_pattern` on one device may be relied on, other than what follows from the above.
Results may differ from the reference program's by a relative error of at most 0.0003.
Values may be sent and summed in bfloat16 or wider, within the bound.
A program may use at most 64 MiB of HBM per device.

```python
import jax
import jax.numpy as jnp

BPD = 4
MOST = 4
NB = 16
ORDER = 2048


def tile_pattern(key):
    tiles = NB // BPD
    count = tiles * tiles
    keys = jax.random.split(jax.random.fold_in(key, 11), count)
    ranks = jax.vmap(lambda k: jax.random.permutation(k, BPD * BPD))(keys)
    counts = jax.random.randint(jax.random.fold_in(key, 12), (count,), 1, MOST + 1)
    chosen = jax.random.randint(jax.random.fold_in(key, 13), (), 0, count)
    counts = jnp.where(jnp.arange(count) == chosen, MOST, counts)
    stored = (ranks < counts[:, None]).astype(jnp.int32)
    stored = stored.reshape(tiles, tiles, BPD, BPD).transpose(0, 2, 1, 3)
    return stored.reshape(NB, NB)


def draw_iterate_pattern(key, part):
    key = jax.random.fold_in(key, 3)
    return tile_pattern(key)


def draw_square_pattern(key, part):
    key = jax.random.fold_in(key, 5)
    return tile_pattern(key)


def place_ends(drawn, key, smallest, top_value):
    longest = drawn.shape.index(max(drawn.shape))
    spots = []
    for shift in (0, 1):
        where = [jax.random.randint(jax.random.fold_in(key, axis), (), 0, length) for axis, length in enumerate(drawn.shape)]
        where[longest] = (where[longest] + shift) % drawn.shape[longest]
        spots.append(tuple(where))
    return drawn.at[spots[0]].set(smallest).at[spots[1]].set(top_value)


def level_of(stream_key, shape, cuts, smallest, largest):
    def one(axis_at, shards_of):
        draws = jax.random.uniform(jax.random.fold_in(jax.random.fold_in(stream_key, 6), axis_at), (shards_of,), jnp.float32, smallest / len(cuts), largest / len(cuts))
        return jnp.repeat(jnp.exp(draws), shape[axis_at] // shards_of).reshape((-1,) + (1,) * (len(shape) - axis_at - 1))

    level = one(*cuts[0])
    for cut in cuts[1:]:
        level = level * one(*cut)
    return level


def normal_values(rng, shape, deviation, reach, shards=(), kind=jnp.bfloat16):
    factor_of = level_of(rng, shape, shards, -0.22, 0.18) if shards else 1.0
    array = jax.random.normal(rng, shape, jnp.float32) * deviation * factor_of
    return jnp.minimum(jnp.maximum(array, -reach), reach).astype(kind)


def setup_inputs(seed: int = 0, part: int = 0) -> dict:
    streams_of = jax.random.split(jax.random.key(seed), 6)
    own_keys = jax.random.split(jax.random.fold_in(streams_of[5], part), 6)
    return {
        "iterate": normal_values(own_keys[0], (ORDER, ORDER), 1.0, 6.0, ((0, 4), (1, 4))),
        "square": normal_values(own_keys[1], (ORDER, ORDER), (ORDER * MOST // (BPD * BPD * 4)) ** -0.5, 0.5, ((0, 4), (1, 4))),
        "iterate_pattern": draw_iterate_pattern(jax.random.fold_in(jax.random.fold_in(streams_of[5], part), 71), part),
        "square_pattern": draw_square_pattern(jax.random.fold_in(jax.random.fold_in(streams_of[5], part), 71), part),
        "keep_pattern": place_ends((jax.random.randint(own_keys[4], (NB, NB), 0, 4) < 3).astype(jnp.int32), jax.random.fold_in(own_keys[4], 1), 0, 1),
    }


def expand(values, pattern):
    block = values.shape[0] // pattern.shape[0]
    full = jnp.repeat(jnp.repeat(pattern, block, axis=0), block, axis=1)
    return values * full.astype(values.dtype)


def reference(iterate, square, iterate_pattern, square_pattern, keep_pattern):
    sparse_x = expand(iterate, iterate_pattern)
    sparse_sq = expand(square, square_pattern)
    product = jnp.dot(sparse_x, sparse_sq, preferred_element_type=jnp.float32)
    update = 1.5 * sparse_x.astype(jnp.float32) - 0.5 * product
    return expand(update, keep_pattern)
```

```python
import functools

import jax
import jax.numpy as jnp
from jax import lax
from jax.experimental import pallas as pl
from jax.experimental.pallas import tpu as pltpu
from jax.sharding import PartitionSpec as P

MESH = pl.DeviceIdType.MESH
BLOCKS = 4
MOST = 4
SIZE = 128
CHUNKS = 2
PER = MOST // CHUNKS


def rows_of(i):
    return pl.ds(i * SIZE, SIZE)


def pack(tile_ref, pattern_ref, packed_ref):
    slots = [jnp.zeros((SIZE, SIZE), packed_ref.dtype)] * MOST
    count = jnp.int32(0)
    for b in range(BLOCKS * BLOCKS):
        i, j = b // BLOCKS, b % BLOCKS
        stored = pattern_ref[i, j]
        block = tile_ref[rows_of(i), rows_of(j)]
        for a in range(min(MOST, b + 1)):
            slots[a] = jnp.where((stored > 0) & (count == a), block, slots[a])
        count = count + stored
    for a in range(MOST):
        packed_ref[a] = slots[a]


def unpack(packed_ref, pattern_ref, at, held, dense_ref):
    held[...] = packed_ref[at]
    count = jnp.int32(0)
    for b in range(BLOCKS * BLOCKS):
        i, j = b // BLOCKS, b % BLOCKS
        stored = pattern_ref[at, i, j]
        block = held[jnp.minimum(count, MOST - 1)]
        dense_ref[rows_of(i), rows_of(j)] = jnp.where(stored > 0, block, jnp.zeros_like(block))
        count = count + stored


def kernel(
    nr, nc, xpat_ref, spat_ref, keep_ref, x_ref, s_ref, out_ref,
    xt, st, xp, sp, xh, sh, xd, sd, acc, xpats, spats,
    load_sem, patx_send, patx_recv, pats_send, pats_recv,
    x_send, x_recv, s_up, s_down, s_recv,
):
    r = lax.axis_index("rows")
    c = lax.axis_index("cols")

    load_s = pltpu.make_async_copy(s_ref, st, load_sem.at[0])
    load_x = pltpu.make_async_copy(x_ref, xt, load_sem.at[1])
    load_s.start()
    load_x.start()

    barrier = pltpu.get_barrier_semaphore()
    for d in range(1, nr):
        pl.semaphore_signal(barrier, inc=1, device_id={"rows": lax.rem(r + d, nr)}, device_id_type=MESH)
    for d in range(1, nc):
        pl.semaphore_signal(barrier, inc=1, device_id={"cols": lax.rem(c + d, nc)}, device_id_type=MESH)
    for i in range(BLOCKS):
        for j in range(BLOCKS):
            xpats[c, i, j] = xpat_ref[i, j]
            spats[r, i, j] = spat_ref[i, j]
    load_s.wait()
    pack(st, spat_ref, sp.at[r])
    pl.semaphore_wait(barrier, nr + nc - 2)

    def s_copy(at, chunk, step, sems):
        piece = sp.at[at, pl.ds(chunk * PER, PER)]
        return pltpu.make_async_remote_copy(
            src_ref=piece, dst_ref=piece, send_sem=sems.at[at, chunk], recv_sem=s_recv.at[at, chunk],
            device_id={"rows": r + step}, device_id_type=MESH,
        )

    def pass_on(at, chunk, up, down):
        @pl.when(up)
        def _():
            s_copy(at, chunk, 1, s_up).start()

        @pl.when(down)
        def _():
            s_copy(at, chunk, -1, s_down).start()

    for chunk in range(CHUNKS):
        pass_on(r, chunk, r < nr - 1, r > 0)

    pattern_copies = []
    for d in range(1, nr):
        pattern_copies.append(pltpu.make_async_remote_copy(
            src_ref=spats.at[r], dst_ref=spats.at[r], send_sem=pats_send.at[d], recv_sem=pats_recv.at[d],
            device_id={"rows": lax.rem(r + d, nr)}, device_id_type=MESH))
    for d in range(1, nc):
        pattern_copies.append(pltpu.make_async_remote_copy(
            src_ref=xpats.at[c], dst_ref=xpats.at[c], send_sem=patx_send.at[d], recv_sem=patx_recv.at[d],
            device_id={"cols": lax.rem(c + d, nc)}, device_id_type=MESH))
    for copy in pattern_copies:
        copy.start()

    load_x.wait()
    pack(xt, xpat_ref, xp.at[c])
    x_copies = []
    for d in range(1, nc):
        x_copies.append(pltpu.make_async_remote_copy(
            src_ref=xp.at[c], dst_ref=xp.at[c], send_sem=x_send.at[d], recv_sem=x_recv.at[d],
            device_id={"cols": lax.rem(c + d, nc)}, device_id_type=MESH))
    for copy in x_copies:
        copy.start()

    def multiply(at, first):
        unpack(xp, xpats, at, xh, xd)
        unpack(sp, spats, at, sh, sd)
        half = sd.shape[1] // 2
        for h in range(2):
            part = pl.ds(h * half, half)
            value = jnp.dot(xd[...], sd[:, part], preferred_element_type=jnp.float32)
            acc[:, part] = value if first else acc[:, part] + value

    acc[...] = jnp.zeros_like(acc)
    for copy in pattern_copies:
        copy.wait()
    for copy in x_copies:
        copy.wait()

    def s_step(step, carry):
        below = r - step
        above = r + step
        has_below = (below >= 0) & (step > 0)
        has_above = above < nr

        for chunk in range(CHUNKS):
            @pl.when(has_below)
            def _():
                s_copy(below, chunk, 1, s_up).wait_recv()
                pass_on(below, chunk, r < nr - 1, False)

            @pl.when(has_above & (step > 0))
            def _():
                s_copy(above, chunk, -1, s_down).wait_recv()
                pass_on(above, chunk, False, r > 0)

        def side(k, carry):
            at = jnp.where(k == 0, below, above)

            @pl.when(jnp.where(k == 0, has_below, has_above))
            def _():
                multiply(at, False)
            return carry

        return lax.fori_loop(0, 2, side, carry)

    lax.fori_loop(0, nr, s_step, 0)

    for i in range(BLOCKS):
        for j in range(BLOCKS):
            x = xt[rows_of(i), rows_of(j)].astype(jnp.float32)
            x = jnp.where(xpat_ref[i, j] > 0, x, 0.0)
            update = 1.5 * x - 0.5 * acc[rows_of(i), rows_of(j)]
            out_ref[rows_of(i), rows_of(j)] = jnp.where(keep_ref[i, j] > 0, update, 0.0)

    def drain(at, carry):
        for chunk in range(CHUNKS):
            @pl.when((at <= r) & (r < nr - 1))
            def _():
                s_copy(at, chunk, 1, s_up).wait_send()

            @pl.when((at >= r) & (r > 0))
            def _():
                s_copy(at, chunk, -1, s_down).wait_send()
        return carry

    lax.fori_loop(0, nr, drain, 0)


def per_device(iterate, square, iterate_pattern, square_pattern, keep_pattern, *, nr, nc):
    order = iterate.shape[0]
    smem = pl.BlockSpec(memory_space=pltpu.SMEM)
    anywhere = pl.BlockSpec(memory_space=pl.ANY)
    dma = pltpu.SemaphoreType.DMA
    return pl.pallas_call(
        functools.partial(kernel, nr, nc),
        out_shape=jax.ShapeDtypeStruct(iterate.shape, jnp.float32),
        in_specs=[smem, smem, smem, anywhere, anywhere],
        out_specs=pl.BlockSpec(memory_space=pltpu.VMEM),
        scratch_shapes=[
            pltpu.VMEM((order, order), jnp.bfloat16),
            pltpu.VMEM((order, order), jnp.bfloat16),
            pltpu.VMEM((nc, MOST, SIZE, SIZE), jnp.bfloat16),
            pltpu.VMEM((nr, MOST, SIZE, SIZE), jnp.bfloat16),
            pltpu.VMEM((MOST, SIZE, SIZE), jnp.bfloat16),
            pltpu.VMEM((MOST, SIZE, SIZE), jnp.bfloat16),
            pltpu.VMEM((order, order), jnp.bfloat16),
            pltpu.VMEM((order, order), jnp.bfloat16),
            pltpu.VMEM((order, order), jnp.float32),
            pltpu.SMEM((nc, BLOCKS, BLOCKS), jnp.int32),
            pltpu.SMEM((nr, BLOCKS, BLOCKS), jnp.int32),
            dma((2,)), dma((nc,)), dma((nc,)), dma((nr,)), dma((nr,)),
            dma((nc,)), dma((nc,)), dma((nr, CHUNKS)), dma((nr, CHUNKS)), dma((nr, CHUNKS)),
        ],
        compiler_params=pltpu.CompilerParams(
            collective_id=0, has_side_effects=True, vmem_limit_bytes=60 * 2**20
        ),
        cost_estimate=pl.CostEstimate(
            flops=2 * order * order * order * nr, bytes_accessed=4 * order * order * 2, transcendentals=0
        ),
    )(iterate_pattern, square_pattern, keep_pattern, iterate, square)


def solution(mesh):
    spec = P(("groups", "rows"), "cols")
    return jax.shard_map(
        functools.partial(per_device, nr=mesh.shape["rows"], nc=mesh.shape["cols"]),
        mesh=mesh,
        in_specs=(spec,) * 5,
        out_specs=spec,
        check_vma=False,
    )
```

```python
import functools

import jax
import jax.numpy as jnp
from jax import lax
from jax.experimental import pallas as pl
from jax.experimental.pallas import tpu as pltpu
from jax.sharding import PartitionSpec as P

MESH = pl.DeviceIdType.MESH
BLOCKS = 4
MOST = 4
SIZE = 128
CODES = BLOCKS * BLOCKS
PACKED = CODES + MOST * SIZE
CUTS = (0, CODES + 2 * SIZE, PACKED)
CHUNKS = len(CUTS) - 1


def rows_of(i):
    return pl.ds(i * SIZE, SIZE)


def pack(tile_ref, pattern_ref, packed_ref):
    row = lax.broadcasted_iota(jnp.int32, (CODES, SIZE), 0)
    codes = jnp.zeros((CODES, SIZE), jnp.int32)
    slots = [jnp.zeros((SIZE, SIZE), packed_ref.dtype)] * MOST
    count = jnp.int32(0)
    for b in range(CODES):
        i, j = b // BLOCKS, b % BLOCKS
        stored = pattern_ref[i, j]
        block = tile_ref[rows_of(i), rows_of(j)]
        for a in range(min(MOST, b + 1)):
            slots[a] = jnp.where((stored > 0) & (count == a), block, slots[a])
        count = count + stored
        codes = jnp.where(row == b, stored * count, codes)
    packed_ref[pl.ds(0, CODES), :] = codes.astype(jnp.float32).astype(packed_ref.dtype)
    for a in range(MOST):
        packed_ref[pl.ds(CODES + a * SIZE, SIZE), :] = slots[a]


def unpack(packed_ref, dense_ref):
    kind = dense_ref.dtype
    codes = packed_ref[pl.ds(0, CODES), :].astype(jnp.float32)
    weights = [jnp.where(codes == a + 1.0, 1.0, 0.0) for a in range(MOST)]
    for b in range(CODES):
        i, j = b // BLOCKS, b % BLOCKS
        block = None
        for a in range(min(MOST, b + 1)):
            weight = jnp.broadcast_to(weights[a][b:b + 1, :], (16, SIZE)).astype(kind)
            slot = packed_ref[pl.ds(CODES + a * SIZE, SIZE), :].reshape(SIZE // 16, 16, SIZE)
            term = slot * weight[None]
            block = term if block is None else block + term
        dense_ref[rows_of(i), rows_of(j)] = block.reshape(SIZE, SIZE)


def kernel(
    nr, nc, xpat_hbm, spat_hbm, keep_hbm, x_hbm, s_hbm, out_hbm,
    xt, st, xp, sp, xd, sd, acc, out, xpat, spat, keep,
    load_sem, out_sem, x_send, x_recv, s_up, s_down, s_recv,
):
    r = lax.axis_index("rows")
    c = lax.axis_index("cols")
    top = r > 0
    bottom = r < nr - 1

    barrier = pltpu.get_barrier_semaphore()

    @pl.when(top)
    def _():
        pl.semaphore_signal(barrier, inc=1, device_id={"rows": r - 1}, device_id_type=MESH)

    @pl.when(bottom)
    def _():
        pl.semaphore_signal(barrier, inc=1, device_id={"rows": r + 1}, device_id_type=MESH)

    for d in range(1, nc):
        pl.semaphore_signal(barrier, inc=1, device_id={"cols": lax.rem(c + d, nc)}, device_id_type=MESH)

    pairs = ((spat_hbm, spat), (s_hbm, st), (xpat_hbm, xpat), (x_hbm, xt), (keep_hbm, keep))
    loads = [pltpu.make_async_copy(a, b, load_sem.at[k]) for k, (a, b) in enumerate(pairs)]
    for load in loads:
        load.start()

    def s_copy(at, chunk, step, sems):
        piece = sp.at[at, pl.ds(CUTS[chunk], CUTS[chunk + 1] - CUTS[chunk])]
        return pltpu.make_async_remote_copy(
            src_ref=piece, dst_ref=piece, send_sem=sems.at[at, chunk], recv_sem=s_recv.at[at, chunk],
            device_id={"rows": r + step}, device_id_type=MESH,
        )

    def pass_on(at, chunk, down, up):
        @pl.when(down)
        def _():
            s_copy(at, chunk, 1, s_down).start()

        @pl.when(up)
        def _():
            s_copy(at, chunk, -1, s_up).start()

    loads[0].wait()
    loads[1].wait()
    pack(st, spat, sp.at[r])
    pl.semaphore_wait(barrier, nc - 1 + top.astype(jnp.int32) + bottom.astype(jnp.int32))
    for chunk in range(CHUNKS):
        pass_on(r, chunk, bottom, top)

    loads[2].wait()
    loads[3].wait()
    pack(xt, xpat, xp.at[c])

    def x_copy(at, to):
        return pltpu.make_async_remote_copy(
            src_ref=xp.at[at], dst_ref=xp.at[at], send_sem=x_send.at[to], recv_sem=x_recv.at[at],
            device_id={"cols": to}, device_id_type=MESH,
        )

    for d in range(1, nc):
        x_copy(c, lax.rem(c + d, nc)).start()

    def arrive(step):
        above = r - step
        below = r + step
        for chunk in range(CHUNKS):
            @pl.when(above >= 0)
            def _():
                s_copy(above, chunk, 1, s_down).wait_recv()
                pass_on(above, chunk, bottom, False)

            @pl.when(below < nr)
            def _():
                s_copy(below, chunk, -1, s_up).wait_recv()
                pass_on(below, chunk, False, top)

    def early(step, carry):
        arrive(step)
        return carry

    lax.fori_loop(1, 3, early, 0)

    def x_tile(at, carry):
        @pl.when(at != c)
        def _():
            x_copy(at, c).wait_recv()

        unpack(xp.at[at], xd.at[at])
        return carry

    lax.fori_loop(0, nc, x_tile, 0)
    acc[...] = jnp.zeros_like(acc)

    def multiply(at):
        unpack(sp.at[at], sd)
        half = sd.shape[1] // 2
        for h in range(2):
            part = pl.ds(h * half, half)
            acc[:, part] += jnp.dot(xd[at], sd[:, part], preferred_element_type=jnp.float32)

    def s_step(step, carry):
        @pl.when(step >= 3)
        def _():
            arrive(step)

        def side(k, carry):
            at = r + (2 * k - 1) * step

            @pl.when((at >= 0) & (at < nr) & (k + step > 0))
            def _():
                multiply(at)
            return carry

        return lax.fori_loop(0, 2, side, carry)

    lax.fori_loop(0, nr, s_step, 0)

    loads[4].wait()
    writes = []
    for i in range(BLOCKS):
        for j in range(BLOCKS):
            x = xt[rows_of(i), rows_of(j)].astype(jnp.float32)
            x = jnp.where(xpat[i, j] > 0, x, 0.0)
            update = 1.5 * x - 0.5 * acc[rows_of(i), rows_of(j)]
            out[rows_of(i), rows_of(j)] = jnp.where(keep[i, j] > 0, update, 0.0)
        writes.append(pltpu.make_async_copy(out.at[rows_of(i)], out_hbm.at[rows_of(i)], out_sem.at[i]))
        writes[-1].start()

    for d in range(1, nc):
        x_copy(c, lax.rem(c + d, nc)).wait_send()

    def drain(at, carry):
        for chunk in range(CHUNKS):
            @pl.when((at <= r) & bottom)
            def _():
                s_copy(at, chunk, 1, s_down).wait_send()

            @pl.when((at >= r) & top)
            def _():
                s_copy(at, chunk, -1, s_up).wait_send()
        return carry

    lax.fori_loop(0, nr, drain, 0)
    for write in writes:
        write.wait()


def per_device(iterate, square, iterate_pattern, square_pattern, keep_pattern, *, nr, nc):
    order = iterate.shape[0]
    anywhere = pl.BlockSpec(memory_space=pl.ANY)
    dma = pltpu.SemaphoreType.DMA
    half = iterate.dtype
    return pl.pallas_call(
        functools.partial(kernel, nr, nc),
        out_shape=jax.ShapeDtypeStruct(iterate.shape, jnp.float32),
        in_specs=[anywhere] * 5,
        out_specs=anywhere,
        scratch_shapes=[
            pltpu.VMEM((order, order), half),
            pltpu.VMEM((order, order), half),
            pltpu.VMEM((nc, PACKED, SIZE), half),
            pltpu.VMEM((nr, PACKED, SIZE), half),
            pltpu.VMEM((nc, order, order), half),
            pltpu.VMEM((order, order), half),
            pltpu.VMEM((order, order), jnp.float32),
            pltpu.VMEM((order, order), jnp.float32),
            pltpu.SMEM((BLOCKS, BLOCKS), jnp.int32),
            pltpu.SMEM((BLOCKS, BLOCKS), jnp.int32),
            pltpu.SMEM((BLOCKS, BLOCKS), jnp.int32),
            dma((5,)), dma((BLOCKS,)), dma((nc,)), dma((nc,)),
            dma((nr, CHUNKS)), dma((nr, CHUNKS)), dma((nr, CHUNKS)),
        ],
        compiler_params=pltpu.CompilerParams(
            collective_id=0, has_side_effects=True, vmem_limit_bytes=60 * 2**20
        ),
        cost_estimate=pl.CostEstimate(
            flops=2 * order * order * order * nr, bytes_accessed=4 * order * order * 2, transcendentals=0
        ),
    )(iterate_pattern, square_pattern, keep_pattern, iterate, square)


def solution(mesh):
    spec = P(("groups", "rows"), "cols")
    return jax.shard_map(
        functools.partial(per_device, nr=mesh.shape["rows"], nc=mesh.shape["cols"]),
        mesh=mesh,
        in_specs=(spec,) * 5,
        out_specs=spec,
        check_vma=False,
    )
```

```python
import functools

import jax
import jax.numpy as jnp
from jax import lax
from jax.experimental import pallas as pl
from jax.experimental.pallas import tpu as pltpu
from jax.sharding import PartitionSpec as P

MESH = pl.DeviceIdType.MESH
PIECES = 4
BLOCKS = 4
MOST = 4
SIZE = 128
CODES = BLOCKS * BLOCKS
PACKED = CODES + MOST * SIZE
CUTS = (0, CODES + SIZE, CODES + 2 * SIZE, CODES + 3 * SIZE, PACKED)
CHUNKS = len(CUTS) - 1
X_CUTS = (0, PACKED)
X_CHUNKS = len(X_CUTS) - 1


def rows_of(i):
    return pl.ds(i * SIZE, SIZE)


def pack(tile_ref, pattern_ref, packed_ref):
    row = lax.broadcasted_iota(jnp.int32, (CODES, SIZE), 0)
    codes = jnp.zeros((CODES, SIZE), jnp.int32)
    slots = [jnp.zeros((SIZE, SIZE), packed_ref.dtype)] * MOST
    count = jnp.int32(0)
    for b in range(CODES):
        i, j = b // BLOCKS, b % BLOCKS
        stored = pattern_ref[i, j]
        block = tile_ref[rows_of(i), rows_of(j)]
        for a in range(min(MOST, b + 1)):
            slots[a] = jnp.where((stored > 0) & (count == a), block, slots[a])
        count = count + stored
        codes = jnp.where(row == b, stored * count, codes)
    packed_ref[pl.ds(0, CODES), :] = codes.astype(jnp.float32).astype(packed_ref.dtype)
    for a in range(MOST):
        packed_ref[pl.ds(CODES + a * SIZE, SIZE), :] = slots[a]


def unpack(packed_ref, dense_ref):
    kind = dense_ref.dtype
    codes = packed_ref[pl.ds(0, CODES), :].astype(jnp.float32)
    weights = [jnp.where(codes == a + 1.0, 1.0, 0.0) for a in range(MOST)]
    for b in range(CODES):
        i, j = b // BLOCKS, b % BLOCKS
        block = None
        for a in range(min(MOST, b + 1)):
            weight = jnp.broadcast_to(weights[a][b:b + 1, :], (16, SIZE)).astype(kind)
            slot = packed_ref[pl.ds(CODES + a * SIZE, SIZE), :].reshape(SIZE // 16, 16, SIZE)
            term = slot * weight[None]
            block = term if block is None else block + term
        dense_ref[rows_of(i), rows_of(j)] = block.reshape(SIZE, SIZE)


def kernel(
    nr, nc, xpat_hbm, spat_hbm, keep_hbm, x_hbm, s_hbm, out_hbm,
    xt, st, xp, sp, xd, sd, acc, out, xpat, spat, keep,
    load_sem, out_sem, x_far, x_near, x_recv, s_up, s_down, s_recv,
):
    r = lax.axis_index("rows")
    c = lax.axis_index("cols")
    chips = nc // 2
    core = lax.rem(c, 2)
    chip = lax.div(c, 2)
    partner = c + 1 - 2 * core
    top = r > 0
    bottom = r < nr - 1

    def same_core(d):
        return 2 * lax.rem(chip + d, chips) + core

    barrier = pltpu.get_barrier_semaphore()

    @pl.when(top)
    def _():
        pl.semaphore_signal(barrier, inc=1, device_id={"rows": r - 1}, device_id_type=MESH)

    @pl.when(bottom)
    def _():
        pl.semaphore_signal(barrier, inc=1, device_id={"rows": r + 1}, device_id_type=MESH)

    pl.semaphore_signal(barrier, inc=1, device_id={"cols": partner}, device_id_type=MESH)
    for d in range(1, chips):
        pl.semaphore_signal(barrier, inc=1, device_id={"cols": same_core(d)}, device_id_type=MESH)

    pairs = ((spat_hbm, spat), (s_hbm, st), (xpat_hbm, xpat), (x_hbm, xt), (keep_hbm, keep))
    loads = [pltpu.make_async_copy(a, b, load_sem.at[k]) for k, (a, b) in enumerate(pairs)]
    for load in loads[:2]:
        load.start()

    def s_copy(at, chunk, step, sems):
        piece = sp.at[at, pl.ds(CUTS[chunk], CUTS[chunk + 1] - CUTS[chunk])]
        return pltpu.make_async_remote_copy(
            src_ref=piece, dst_ref=piece, send_sem=sems.at[at, chunk], recv_sem=s_recv.at[at, chunk],
            device_id={"rows": r + step}, device_id_type=MESH,
        )

    def pass_on(at, chunk, down, up):
        @pl.when(up)
        def _():
            s_copy(at, chunk, -1, s_up).start()

        @pl.when(down)
        def _():
            s_copy(at, chunk, 1, s_down).start()

    loads[0].wait()
    loads[1].wait()
    for load in loads[2:]:
        load.start()
    pack(st, spat, sp.at[r])
    pl.semaphore_wait(barrier, chips + top.astype(jnp.int32) + bottom.astype(jnp.int32))
    for chunk in range(CHUNKS):
        pass_on(r, chunk, bottom, top)

    loads[2].wait()
    loads[3].wait()
    pack(xt, xpat, xp.at[c])

    def x_copy(at, chunk, to, send_sem):
        piece = xp.at[at, pl.ds(X_CUTS[chunk], X_CUTS[chunk + 1] - X_CUTS[chunk])]
        return pltpu.make_async_remote_copy(
            src_ref=piece, dst_ref=piece, send_sem=send_sem, recv_sem=x_recv.at[at, chunk],
            device_id={"cols": to}, device_id_type=MESH,
        )

    def to_far(d, chunk):
        return x_copy(c, chunk, same_core(d), x_far.at[d, chunk])

    def to_partner(at, chunk):
        return x_copy(at, chunk, partner, x_near.at[at, chunk])

    for chunk in range(X_CHUNKS):
        for d in range(1, chips):
            to_far(d, chunk).start()
    for chunk in range(X_CHUNKS):
        to_partner(c, chunk).start()

    def arrive(step):
        above = r - step
        below = r + step
        for chunk in range(CHUNKS):
            @pl.when(above >= 0)
            def _():
                s_copy(above, chunk, 1, s_down).wait_recv()
                pass_on(above, chunk, bottom, False)

            @pl.when(below < nr)
            def _():
                s_copy(below, chunk, -1, s_up).wait_recv()
                pass_on(below, chunk, False, top)

    between = top & bottom
    arrive(1)

    @pl.when(between)
    def _():
        arrive(2)

    for chunk in range(X_CHUNKS):
        for d in range(1, chips):
            to_partner(same_core(d), chunk).wait_recv()
            to_partner(same_core(d), chunk).start()

    def x_tile(d, carry):
        mine = same_core(d)
        other = mine + 1 - 2 * core

        unpack(xp.at[mine], xd.at[mine])
        for chunk in range(X_CHUNKS):
            to_partner(other, chunk).wait_recv()
        unpack(xp.at[other], xd.at[other])
        return carry

    lax.fori_loop(0, chips, x_tile, 0)
    acc[...] = jnp.zeros_like(acc)

    def multiply(at):
        unpack(sp.at[at], sd)
        half = sd.shape[1] // 2
        for h in range(2):
            part = pl.ds(h * half, half)
            acc[:, part] += jnp.dot(xd[at], sd[:, part], preferred_element_type=jnp.float32)

    def s_step(step, carry):
        ahead = step + between.astype(jnp.int32)

        @pl.when(ahead >= 2 + between.astype(jnp.int32))
        def _():
            arrive(ahead)

        def side(k, carry):
            at = r + (2 * k - 1) * step

            @pl.when((at >= 0) & (at < nr) & (k + step > 0))
            def _():
                multiply(at)
            return carry

        return lax.fori_loop(0, 2, side, carry)

    lax.fori_loop(0, nr, s_step, 0)

    loads[4].wait()
    writes = []
    for i in range(BLOCKS):
        for j in range(BLOCKS):
            x = xt[rows_of(i), rows_of(j)].astype(jnp.float32)
            x = jnp.where(xpat[i, j] > 0, x, 0.0)
            update = 1.5 * x - 0.5 * acc[rows_of(i), rows_of(j)]
            out[rows_of(i), rows_of(j)] = jnp.where(keep[i, j] > 0, update, 0.0)
        writes.append(pltpu.make_async_copy(out.at[rows_of(i)], out_hbm.at[rows_of(i)], out_sem.at[i]))
        writes[-1].start()

    for chunk in range(X_CHUNKS):
        for d in range(1, chips):
            to_far(d, chunk).wait_send()
        for d in range(chips):
            to_partner(same_core(d), chunk).wait_send()

    def drain(at, carry):
        for chunk in range(CHUNKS):
            @pl.when((at <= r) & bottom)
            def _():
                s_copy(at, chunk, 1, s_down).wait_send()

            @pl.when((at >= r) & top)
            def _():
                s_copy(at, chunk, -1, s_up).wait_send()
        return carry

    lax.fori_loop(0, nr, drain, 0)
    for write in writes:
        write.wait()


def hand_over(from_ref, to_ref, held, sems):
    size = held.shape[0] // PIECES
    pieces = [pl.ds(k * size, size) for k in range(PIECES)]
    reads = [pltpu.make_async_copy(from_ref.at[p], held.at[p], sems.at[0, k]) for k, p in enumerate(pieces)]
    writes = [pltpu.make_async_copy(held.at[p], to_ref.at[p], sems.at[1, k]) for k, p in enumerate(pieces)]
    for read in reads:
        read.start()
    for read, write in zip(reads, writes):
        read.wait()
        write.start()
    for write in writes:
        write.wait()


def per_device(iterate, square, iterate_pattern, square_pattern, keep_pattern, *, nr, nc):
    order = iterate.shape[0]
    anywhere = pl.BlockSpec(memory_space=pl.ANY)
    dma = pltpu.SemaphoreType.DMA
    half = iterate.dtype
    result = pl.pallas_call(
        functools.partial(kernel, nr, nc),
        out_shape=jax.ShapeDtypeStruct(iterate.shape, jnp.float32),
        in_specs=[anywhere] * 5,
        out_specs=anywhere,
        scratch_shapes=[
            pltpu.VMEM((order, order), half),
            pltpu.VMEM((order, order), half),
            pltpu.VMEM((nc, PACKED, SIZE), half),
            pltpu.VMEM((nr, PACKED, SIZE), half),
            pltpu.VMEM((nc, order, order), half),
            pltpu.VMEM((order, order), half),
            pltpu.VMEM((order, order), jnp.float32),
            pltpu.VMEM((order, order), jnp.float32),
            pltpu.SMEM((BLOCKS, BLOCKS), jnp.int32),
            pltpu.SMEM((BLOCKS, BLOCKS), jnp.int32),
            pltpu.SMEM((BLOCKS, BLOCKS), jnp.int32),
            dma((5,)), dma((BLOCKS,)), dma((nc // 2, X_CHUNKS)), dma((nc, X_CHUNKS)), dma((nc, X_CHUNKS)),
            dma((nr, CHUNKS)), dma((nr, CHUNKS)), dma((nr, CHUNKS)),
        ],
        compiler_params=pltpu.CompilerParams(
            collective_id=0, has_side_effects=True, vmem_limit_bytes=60 * 2**20
        ),
        cost_estimate=pl.CostEstimate(
            flops=2 * order * order * order * nr, bytes_accessed=4 * order * order * 2, transcendentals=0
        ),
    )(iterate_pattern, square_pattern, keep_pattern, iterate, square)
    return pl.pallas_call(
        hand_over,
        out_shape=jax.ShapeDtypeStruct(iterate.shape, jnp.float32),
        in_specs=[anywhere],
        out_specs=anywhere,
        scratch_shapes=[pltpu.VMEM((order, order), jnp.float32), dma((2, PIECES))],
        compiler_params=pltpu.CompilerParams(vmem_limit_bytes=60 * 2**20),
    )(result)


def solution(mesh):
    spec = P(("groups", "rows"), "cols")
    return jax.shard_map(
        functools.partial(per_device, nr=mesh.shape["rows"], nc=mesh.shape["cols"]),
        mesh=mesh,
        in_specs=(spec,) * 5,
        out_specs=spec,
        check_vma=False,
    )
```

```python
import functools

import jax
import jax.numpy as jnp
from jax import lax
from jax.experimental import pallas as pl
from jax.experimental.pallas import tpu as pltpu
from jax.sharding import PartitionSpec as P

MESH = pl.DeviceIdType.MESH
PIECES = 2
BLOCKS = 4
MOST = 4
SIZE = 128
CODES = BLOCKS * BLOCKS
PACKED = CODES + MOST * SIZE
CUTS = (0, CODES + SIZE, CODES + 2 * SIZE, CODES + 3 * SIZE, PACKED)
CHUNKS = len(CUTS) - 1
X_CUTS = (0, PACKED)
X_CHUNKS = len(X_CUTS) - 1


def rows_of(i):
    return pl.ds(i * SIZE, SIZE)


def pack(tile_ref, pattern_ref, packed_ref):
    row = lax.broadcasted_iota(jnp.int32, (CODES, SIZE), 0)
    codes = jnp.zeros((CODES, SIZE), jnp.int32)
    slots = [jnp.zeros((SIZE, SIZE), packed_ref.dtype)] * MOST
    count = jnp.int32(0)
    for b in range(CODES):
        i, j = b // BLOCKS, b % BLOCKS
        stored = pattern_ref[i, j]
        block = tile_ref[rows_of(i), rows_of(j)]
        for a in range(min(MOST, b + 1)):
            slots[a] = jnp.where((stored > 0) & (count == a), block, slots[a])
        count = count + stored
        codes = jnp.where(row == b, stored * count, codes)
    packed_ref[pl.ds(0, CODES), :] = codes.astype(jnp.float32).astype(packed_ref.dtype)
    for a in range(MOST):
        packed_ref[pl.ds(CODES + a * SIZE, SIZE), :] = slots[a]


def unpack(packed_ref, dense_ref):
    kind = dense_ref.dtype
    codes = packed_ref[pl.ds(0, CODES), :].astype(jnp.float32)
    weights = [jnp.where(codes == a + 1.0, 1.0, 0.0) for a in range(MOST)]
    for b in range(CODES):
        i, j = b // BLOCKS, b % BLOCKS
        block = None
        for a in range(min(MOST, b + 1)):
            weight = jnp.broadcast_to(weights[a][b:b + 1, :], (16, SIZE)).astype(kind)
            slot = packed_ref[pl.ds(CODES + a * SIZE, SIZE), :].reshape(SIZE // 16, 16, SIZE)
            term = slot * weight[None]
            block = term if block is None else block + term
        dense_ref[rows_of(i), rows_of(j)] = block.reshape(SIZE, SIZE)


def kernel(
    nr, nc, xpat_hbm, spat_hbm, keep_hbm, x_hbm, s_hbm, out_hbm,
    xt, st, xp, sp, xd, sd, acc, out, xpat, spat, keep,
    load_sem, out_sem, x_far, x_near, x_recv, s_up, s_down, s_recv,
):
    r = lax.axis_index("rows")
    c = lax.axis_index("cols")
    chips = nc // 2
    core = lax.rem(c, 2)
    chip = lax.div(c, 2)
    partner = c + 1 - 2 * core
    top = r > 0
    bottom = r < nr - 1

    def same_core(d):
        return 2 * lax.rem(chip + d, chips) + core

    barrier = pltpu.get_barrier_semaphore()

    @pl.when(top)
    def _():
        pl.semaphore_signal(barrier, inc=1, device_id={"rows": r - 1}, device_id_type=MESH)

    @pl.when(bottom)
    def _():
        pl.semaphore_signal(barrier, inc=1, device_id={"rows": r + 1}, device_id_type=MESH)

    pl.semaphore_signal(barrier, inc=1, device_id={"cols": partner}, device_id_type=MESH)
    for d in range(1, chips):
        pl.semaphore_signal(barrier, inc=1, device_id={"cols": same_core(d)}, device_id_type=MESH)

    pairs = ((spat_hbm, spat), (s_hbm, st), (xpat_hbm, xpat), (x_hbm, xt), (keep_hbm, keep))
    loads = [pltpu.make_async_copy(a, b, load_sem.at[k]) for k, (a, b) in enumerate(pairs)]
    for load in loads[:2]:
        load.start()

    def s_copy(at, chunk, step, sems):
        piece = sp.at[at, pl.ds(CUTS[chunk], CUTS[chunk + 1] - CUTS[chunk])]
        return pltpu.make_async_remote_copy(
            src_ref=piece, dst_ref=piece, send_sem=sems.at[at, chunk], recv_sem=s_recv.at[at, chunk],
            device_id={"rows": r + step}, device_id_type=MESH,
        )

    def pass_on(at, chunk, down, up):
        @pl.when(up)
        def _():
            s_copy(at, chunk, -1, s_up).start()

        @pl.when(down)
        def _():
            s_copy(at, chunk, 1, s_down).start()

    loads[0].wait()
    loads[1].wait()
    for load in loads[2:]:
        load.start()
    pack(st, spat, sp.at[r])
    pl.semaphore_wait(barrier, chips + top.astype(jnp.int32) + bottom.astype(jnp.int32))
    for chunk in range(CHUNKS):
        pass_on(r, chunk, bottom, top)

    loads[2].wait()
    loads[3].wait()
    pack(xt, xpat, xp.at[c])

    def x_copy(at, chunk, to, send_sem):
        piece = xp.at[at, pl.ds(X_CUTS[chunk], X_CUTS[chunk + 1] - X_CUTS[chunk])]
        return pltpu.make_async_remote_copy(
            src_ref=piece, dst_ref=piece, send_sem=send_sem, recv_sem=x_recv.at[at, chunk],
            device_id={"cols": to}, device_id_type=MESH,
        )

    def to_far(d, chunk):
        return x_copy(c, chunk, same_core(d), x_far.at[d, chunk])

    def to_partner(at, chunk):
        return x_copy(at, chunk, partner, x_near.at[at, chunk])

    for chunk in range(X_CHUNKS):
        for d in range(1, chips):
            to_far(d, chunk).start()
    for chunk in range(X_CHUNKS):
        to_partner(c, chunk).start()

    def arrive(step):
        above = r - step
        below = r + step
        for chunk in range(CHUNKS):
            @pl.when(below < nr)
            def _():
                s_copy(below, chunk, -1, s_up).wait_recv()
                pass_on(below, chunk, False, top)

            @pl.when(above >= 0)
            def _():
                s_copy(above, chunk, 1, s_down).wait_recv()
                pass_on(above, chunk, bottom, False)

    between = top & bottom
    arrive(1)

    @pl.when(between)
    def _():
        arrive(2)

    for chunk in range(X_CHUNKS):
        for d in range(1, chips):
            to_partner(same_core(d), chunk).wait_recv()
            to_partner(same_core(d), chunk).start()

    def x_tile(d, carry):
        mine = same_core(d)
        other = mine + 1 - 2 * core

        unpack(xp.at[mine], xd.at[mine])
        for chunk in range(X_CHUNKS):
            to_partner(other, chunk).wait_recv()
        unpack(xp.at[other], xd.at[other])
        return carry

    lax.fori_loop(0, chips, x_tile, 0)
    acc[...] = jnp.zeros_like(acc)

    def multiply(at):
        unpack(sp.at[at], sd)
        acc[...] += jnp.dot(xd[at], sd[...], preferred_element_type=jnp.float32)

    def s_step(step, carry):
        ahead = step + between.astype(jnp.int32)

        @pl.when(ahead >= 2 + between.astype(jnp.int32))
        def _():
            arrive(ahead)

        def side(k, carry):
            at = r + (2 * k - 1) * step

            @pl.when((at >= 0) & (at < nr) & (k + step > 0))
            def _():
                multiply(at)
            return carry

        return lax.fori_loop(0, 2, side, carry)

    lax.fori_loop(0, nr, s_step, 0)

    loads[4].wait()
    writes = []
    for i in range(BLOCKS):
        for j in range(BLOCKS):
            x = xt[rows_of(i), rows_of(j)].astype(jnp.float32)
            x = jnp.where(xpat[i, j] > 0, x, 0.0)
            update = 1.5 * x - 0.5 * acc[rows_of(i), rows_of(j)]
            out[rows_of(i), rows_of(j)] = jnp.where(keep[i, j] > 0, update, 0.0)
        writes.append(pltpu.make_async_copy(out.at[rows_of(i)], out_hbm.at[rows_of(i)], out_sem.at[i]))
        writes[-1].start()

    for chunk in range(X_CHUNKS):
        for d in range(1, chips):
            to_far(d, chunk).wait_send()
        for d in range(chips):
            to_partner(same_core(d), chunk).wait_send()

    def drain(at, carry):
        for chunk in range(CHUNKS):
            @pl.when((at <= r) & bottom)
            def _():
                s_copy(at, chunk, 1, s_down).wait_send()

            @pl.when((at >= r) & top)
            def _():
                s_copy(at, chunk, -1, s_up).wait_send()
        return carry

    lax.fori_loop(0, nr, drain, 0)
    for write in writes:
        write.wait()


def hand_over(from_ref, to_ref, held, sems):
    size = held.shape[0] // PIECES
    pieces = [pl.ds(k * size, size) for k in range(PIECES)]
    reads = [pltpu.make_async_copy(from_ref.at[p], held.at[p], sems.at[0, k]) for k, p in enumerate(pieces)]
    writes = [pltpu.make_async_copy(held.at[p], to_ref.at[p], sems.at[1, k]) for k, p in enumerate(pieces)]
    for read in reads:
        read.start()
    for read, write in zip(reads, writes):
        read.wait()
        write.start()
    for write in writes:
        write.wait()


def per_device(iterate, square, iterate_pattern, square_pattern, keep_pattern, *, nr, nc):
    order = iterate.shape[0]
    anywhere = pl.BlockSpec(memory_space=pl.ANY)
    dma = pltpu.SemaphoreType.DMA
    half = iterate.dtype
    result = pl.pallas_call(
        functools.partial(kernel, nr, nc),
        out_shape=jax.ShapeDtypeStruct(iterate.shape, jnp.float32),
        in_specs=[anywhere] * 5,
        out_specs=anywhere,
        scratch_shapes=[
            pltpu.VMEM((order, order), half),
            pltpu.VMEM((order, order), half),
            pltpu.VMEM((nc, PACKED, SIZE), half),
            pltpu.VMEM((nr, PACKED, SIZE), half),
            pltpu.VMEM((nc, order, order), half),
            pltpu.VMEM((order, order), half),
            pltpu.VMEM((order, order), jnp.float32),
            pltpu.VMEM((order, order), jnp.float32),
            pltpu.SMEM((BLOCKS, BLOCKS), jnp.int32),
            pltpu.SMEM((BLOCKS, BLOCKS), jnp.int32),
            pltpu.SMEM((BLOCKS, BLOCKS), jnp.int32),
            dma((5,)), dma((BLOCKS,)), dma((nc // 2, X_CHUNKS)), dma((nc, X_CHUNKS)), dma((nc, X_CHUNKS)),
            dma((nr, CHUNKS)), dma((nr, CHUNKS)), dma((nr, CHUNKS)),
        ],
        compiler_params=pltpu.CompilerParams(
            collective_id=0, has_side_effects=True, vmem_limit_bytes=60 * 2**20
        ),
        cost_estimate=pl.CostEstimate(
            flops=2 * order * order * order * nr, bytes_accessed=4 * order * order * 2, transcendentals=0
        ),
    )(iterate_pattern, square_pattern, keep_pattern, iterate, square)
    return pl.pallas_call(
        hand_over,
        out_shape=jax.ShapeDtypeStruct(iterate.shape, jnp.float32),
        in_specs=[anywhere],
        out_specs=anywhere,
        scratch_shapes=[pltpu.VMEM((order, order), jnp.float32), dma((2, PIECES))],
        compiler_params=pltpu.CompilerParams(vmem_limit_bytes=60 * 2**20),
    )(result)


def solution(mesh):
    spec = P(("groups", "rows"), "cols")
    return jax.shard_map(
        functools.partial(per_device, nr=mesh.shape["rows"], nc=mesh.shape["cols"]),
        mesh=mesh,
        in_specs=(spec,) * 5,
        out_specs=spec,
        check_vma=False,
    )
```
